32 devices in a mesh: fsdp: 2 (over y), uly: 4 (over x, core), blk: 4 (over z).
Axes of the slice: x: 2, y: 2, z: 4, core: 2. Of those that a mesh axis runs over, the one named last changes fastest.
Arguments:
- latents: bfloat16 [2, 3072, 3072], P('fsdp', ('uly', 'blk')), may hold values from -40 to 40
- sampler_noise: bfloat16 [2, 3072, 3072], P('fsdp', ('uly', 'blk')), may hold values from -6 to 6
- query_key_value_weight: bfloat16 [3, 3072, 1536], P(None, 'fsdp', 'uly'), may hold values from -0.375 to 0.375
- output_weight: bfloat16 [3072, 1536], P('fsdp', 'uly'), may hold values from -0.15625 to 0.15625
- adapter_down_map: bfloat16 [64, 1536], P(None, 'uly'), may hold values from -0.15625 to 0.15625
- adapter_up_map: bfloat16 [64, 3072], replicated, may hold values from -0.75 to 0.75
- valid_token_count: int32 [2], P('fsdp'), may hold values from 1536 to 3072
- advantage: float32 [2], P('fsdp'), may hold values from -3 to 3
- timestep_index: int32 [1], replicated, may hold values from 1 to 15
Outputs:
- next_latents: bfloat16 [2, 3072, 3072], P('fsdp', ('uly', 'blk'))
- log_ratio: float32 [2], P('fsdp')
- grad_down: float32 [64, 1536], P(None, 'uly')
- grad_up: float32 [64, 3072], replicated
The draws below stay inside these ranges and needn't reach their ends.
All inputs are finite; a program needn't handle non-finite values.
Results may differ from the reference program's by a relative error of at most 0.0055.
The reference program's roundings to bfloat16 on the way count: a program that leaves them out, or rounds other values in their place, can miss the bound.
Values may be sent and summed in bfloat16 or wider, within the bound.
A program may use at most 128 MiB of HBM per device.

```python
import math
import jax
import jax.numpy as jnp
from jax import lax

MODEL_WIDTH = 3072
LOCAL_HEADS = 12
HEAD_SIZE = 128
ADAPTER_RANK = 64
STEPS = 16
VIDEOS = 2
SEQ = 3072


def draw_latents(key, part):
    base_key, row_key, col_key = jax.random.split(jax.random.fold_in(key, 21), 3)
    array_shape = (VIDEOS, SEQ, MODEL_WIDTH)
    row_scale = jnp.exp(jax.random.uniform(row_key, (VIDEOS, SEQ, 1), jnp.float32, math.log(0.3), math.log(3.0)))
    col_scale = jnp.exp(jax.random.uniform(col_key, (1, 1, MODEL_WIDTH), jnp.float32, math.log(0.3), math.log(3.0)))
    base = jax.random.normal(base_key, array_shape, jnp.float32)
    return jnp.clip(base * row_scale * col_scale, -40.0, 40.0).astype(jnp.bfloat16)


def draw_query_key_value_weight(key, part):
    base_key = jax.random.fold_in(jax.random.fold_in(key, 7), 0)
    width = LOCAL_HEADS * HEAD_SIZE
    spread = 1.6 / math.sqrt(MODEL_WIDTH)
    base = jax.random.normal(base_key, (3, MODEL_WIDTH, width), jnp.float32) * spread
    return jnp.clip(base, -0.375, 0.375).astype(jnp.bfloat16)


def block_levels(key, shape, pieces, smallest, largest):
    def one(axis_at, blocks):
        heights = jax.random.uniform(jax.random.fold_in(jax.random.fold_in(key, 6), axis_at), (blocks,), jnp.float32, smallest / len(pieces), largest / len(pieces))
        return jnp.repeat(jnp.exp(heights), shape[axis_at] // blocks).reshape((-1,) + (1,) * (len(shape) - axis_at - 1))

    loudness = one(*pieces[0])
    for cut in pieces[1:]:
        loudness = loudness * one(*cut)
    return loudness


def scatter_about(key, shape, scale, bound, shards=(), kind=jnp.bfloat16):
    values = jax.random.normal(key, shape, jnp.float32) * scale
    if len(shards) > 0:
        values = block_levels(key, shape, shards, -0.22, 0.18) * values
    return jnp.clip(values, min=-bound, max=bound).astype(kind)


def setup_inputs(seed: int = 0) -> dict:
    key_of = jax.random.split(jax.random.key(seed), 10)
    latents = draw_latents(jax.random.fold_in(key_of[9], 71), 0)
    sampler_noise = scatter_about(key_of[1], (VIDEOS, SEQ, MODEL_WIDTH), 1.0, 6.0, ((0, 2), (1, 16)))
    query_key_value_weight = draw_query_key_value_weight(jax.random.fold_in(key_of[9], 71), 0)
    output_weight = scatter_about(key_of[3], (MODEL_WIDTH, LOCAL_HEADS * HEAD_SIZE), (LOCAL_HEADS * HEAD_SIZE) ** -0.5, 0.15625, ((0, 2), (1, 4)))
    adapter_down_map = scatter_about(key_of[4], (ADAPTER_RANK, LOCAL_HEADS * HEAD_SIZE), (LOCAL_HEADS * HEAD_SIZE) ** -0.5, 0.15625, ((1, 4),))
    adapter_up_map = scatter_about(key_of[5], (ADAPTER_RANK, MODEL_WIDTH), ADAPTER_RANK ** -0.5, 0.75)
    valid_token_count = jax.random.randint(key_of[6], (VIDEOS,), SEQ // 2, SEQ + 1).astype(jnp.int32)
    advantage = scatter_about(key_of[7], (VIDEOS,), 1.0, 3.0, ((0, 2),), jnp.float32)
    timestep_index = jax.random.randint(key_of[8], (1,), 1, STEPS).astype(jnp.int32)
    return dict(latents=latents, sampler_noise=sampler_noise, query_key_value_weight=query_key_value_weight, output_weight=output_weight, adapter_down_map=adapter_down_map, adapter_up_map=adapter_up_map, valid_token_count=valid_token_count, advantage=advantage, timestep_index=timestep_index)


noise_level = 0.7
loss_scale = 4194304.0
rms_eps = 1e-06

def reference(latents, sampler_noise, query_key_value_weight, output_weight, adapter_down_map, adapter_up_map, valid_token_count, advantage, timestep_index):
    step_float = timestep_index[0].astype(jnp.float32)
    time_now = 1.0 - step_float / STEPS
    step_size = 1.0 / STEPS
    noise_std = noise_level * jnp.sqrt(time_now / (1.0 - time_now))
    drift_gain = 1.0 + noise_level ** 2 / 2.0
    ratio_gain = jnp.sqrt(step_size) * drift_gain / noise_std
    positions = jnp.arange(SEQ, dtype=jnp.int32)

    def one_video(inputs):
        video_lat, video_noise, limit, video_adv = inputs
        current = video_lat.astype(jnp.float32)
        normed = (current * lax.rsqrt(lax.optimization_barrier(jnp.mean(current * current, -1, keepdims=True)) + rms_eps)).astype(jnp.bfloat16)
        query_all = jnp.dot(normed, query_key_value_weight[0], preferred_element_type=jnp.float32).astype(jnp.bfloat16)
        key_all = jnp.dot(normed, query_key_value_weight[1], preferred_element_type=jnp.float32).astype(jnp.bfloat16)
        value_all = jnp.dot(normed, query_key_value_weight[2], preferred_element_type=jnp.float32).astype(jnp.bfloat16)
        key_ok = positions < limit

        def head_attention(head_id):
            start = (head_id * HEAD_SIZE).astype(jnp.int32)
            query_head = lax.dynamic_slice_in_dim(query_all, start, HEAD_SIZE, 1)
            key_head = lax.dynamic_slice_in_dim(key_all, start, HEAD_SIZE, 1)
            value_head = lax.dynamic_slice_in_dim(value_all, start, HEAD_SIZE, 1)
            scores = jnp.dot(query_head, key_head.T, preferred_element_type=jnp.float32) * (1.0 / math.sqrt(HEAD_SIZE))
            masked = jnp.where(key_ok[None, :], scores, -1e+30)
            row_max = lax.optimization_barrier(jnp.max(masked, -1, keepdims=True))
            exp_terms = jnp.where(key_ok[None, :], jnp.exp(masked - row_max), 0.0)
            weights = (exp_terms / lax.optimization_barrier(jnp.sum(exp_terms, -1, keepdims=True))).astype(jnp.bfloat16)
            return jnp.dot(weights, value_head, preferred_element_type=jnp.float32).astype(jnp.bfloat16)
        per_head = lax.map(head_attention, jnp.arange(LOCAL_HEADS, dtype=jnp.int32))
        attention_output = jnp.transpose(per_head, (1, 0, 2)).reshape(SEQ, LOCAL_HEADS * HEAD_SIZE)
        velocity = jnp.dot(attention_output, output_weight.T, preferred_element_type=jnp.float32)
        narrow_projection = jnp.dot(attention_output, adapter_down_map.T, preferred_element_type=jnp.float32).astype(jnp.bfloat16)
        adapter_result = jnp.dot(narrow_projection, adapter_up_map, preferred_element_type=jnp.float32)
        noise_f = video_noise.astype(jnp.float32)
        moved = current - step_size * (drift_gain * velocity + noise_level ** 2 * current / (2.0 * (1.0 - time_now)))
        next_video = (moved + noise_std * jnp.sqrt(step_size) * noise_f).astype(jnp.bfloat16)
        standard = noise_f + ratio_gain * adapter_result
        tok_ok = key_ok[:, None]
        valid_len = limit.astype(jnp.float32)
        ratio_log = jnp.sum(jnp.where(tok_ok, noise_f * noise_f - standard * standard, 0.0)) / (2.0 * valid_len * MODEL_WIDTH)
        coef = loss_scale * video_adv * jnp.exp(ratio_log) * ratio_gain / (VIDEOS * valid_len * MODEL_WIDTH)
        delta_gradient = (jnp.where(tok_ok, standard, 0.0) * coef).astype(jnp.bfloat16)
        up_part = jnp.dot(narrow_projection.T, delta_gradient, preferred_element_type=jnp.float32)
        narrow_gradient = jnp.dot(delta_gradient, adapter_up_map.T, preferred_element_type=jnp.float32).astype(jnp.bfloat16)
        down_part = jnp.dot(narrow_gradient.T, attention_output, preferred_element_type=jnp.float32)
        return (next_video, ratio_log, down_part, up_part)
    next_latents, log_ratio, down_parts, up_parts = lax.map(one_video, (latents, sampler_noise, valid_token_count, advantage))
    return (next_latents, log_ratio, lax.optimization_barrier(jnp.sum(down_parts, 0)), lax.optimization_barrier(jnp.sum(up_parts, 0)))
```

```python
import math

import jax
import jax.numpy as jnp
from jax import lax
from jax.sharding import PartitionSpec as P

HEAD_SIZE = 128
STEPS = 16


noise_level = 0.7
loss_scale = 4194304.0
rms_eps = 1e-06


def shift(x, axis, by):
    n = lax.axis_size(axis)
    return lax.ppermute(x, axis, [((i + by) % n, i) for i in range(n)])


def swap(x, axis, bit):
    n = lax.axis_size(axis)
    return lax.ppermute(x, axis, [(i ^ bit, i) for i in range(n)])


def bits_of(axis):
    n = lax.axis_size(axis)
    assert n & (n - 1) == 0
    return [1 << i for i in reversed(range(n.bit_length() - 1))]


def xor_gather(x, axis):
    blocks = {0: x}
    for bit in bits_of(axis):
        got = {j ^ bit: swap(v, axis, bit) for j, v in blocks.items()}
        blocks.update(got)
    return [blocks[j] for j in range(lax.axis_size(axis))]


def xor_scatter(blocks, axis):
    held = dict(enumerate(blocks))
    for bit in reversed(bits_of(axis)):
        got = {j ^ bit: swap(v, axis, bit) for j, v in held.items() if j & bit}
        held = {j: held[j] + got[j] for j in got}
    return held[0]


def turn(blocks, me):
    n = len(blocks)
    if n == 1:
        return blocks
    return [
        lax.select_n(
            lax.rem(c - me + n, n), *blocks
        ) if n > 2 else jnp.where(me == c, blocks[0], blocks[1])
        for c in range(n)
    ]


def shards(
    latents,
    sampler_noise,
    query_key_value_weight,
    output_weight,
    adapter_down_map,
    adapter_up_map,
    valid_token_count,
    advantage,
    timestep_index,
):
    fsdp_count = lax.axis_size("fsdp")
    uly_count = lax.axis_size("uly")
    blk_count = lax.axis_size("blk")
    fsdp_id = lax.axis_index("fsdp")
    uly_id = lax.axis_index("uly")
    blk_id = lax.axis_index("blk")
    weights_by_k = {}
    for j in (1, 2, 0):
        own = query_key_value_weight[j]
        weights_by_k[j] = [own] + [shift(own, "fsdp", k) for k in range(1, fsdp_count)]
    out_parts = [output_weight] + [shift(output_weight, "fsdp", k) for k in range(1, fsdp_count)]

    current = latents[0].astype(jnp.float32)
    rows = current.shape[0]
    width = current.shape[1]
    half = width // fsdp_count
    normed = (current * lax.rsqrt(jnp.mean(current * current, -1, keepdims=True) + rms_eps)).astype(
        jnp.bfloat16
    )
    gathered = jnp.concatenate(xor_gather(normed, "uly"), 0)
    halves = [
        lax.dynamic_slice_in_dim(gathered, lax.rem(fsdp_id + k, fsdp_count) * half, half, 1)
        for k in range(fsdp_count)
    ]

    def project(j):
        total = None
        for part, weight in zip(halves, weights_by_k[j]):
            term = jnp.dot(part, weight, preferred_element_type=jnp.float32)
            total = term if total is None else total + term
        return total.astype(jnp.bfloat16)

    def ring(x):
        blocks = [x]
        for _ in range(blk_count - 1):
            blocks.append(shift(blocks[-1], "blk", 1))
        return blocks

    key_blocks = ring(project(1))
    value_blocks = ring(project(2))
    query_rows = project(0)

    limit = valid_token_count[0]
    group_rows = uly_count * rows
    row_index = jnp.arange(group_rows, dtype=jnp.int32)
    row_uly = jnp.bitwise_xor(row_index // rows, uly_id)
    heads_here = query_rows.shape[1] // HEAD_SIZE

    def split(x):
        return x.reshape(x.shape[0], heads_here, HEAD_SIZE)

    query_split = split(query_rows)
    masked = []
    oks = []
    for step in range(blk_count):
        from_blk = lax.rem(blk_id + step, blk_count)
        pos = (row_uly * blk_count + from_blk) * rows + row_index % rows
        ok = (pos < limit)[None, None, :]
        scores = jnp.einsum(
            "qhd,khd->hqk", query_split, split(key_blocks[step]), preferred_element_type=jnp.float32
        ) * (1.0 / math.sqrt(HEAD_SIZE))
        masked.append(jnp.where(ok, scores, -1e30))
        oks.append(ok)
    row_max = jnp.max(masked[0], -1, keepdims=True)
    for m in masked[1:]:
        row_max = jnp.maximum(row_max, jnp.max(m, -1, keepdims=True))
    terms = [jnp.where(ok, jnp.exp(m - row_max), 0.0) for m, ok in zip(masked, oks)]
    total = jnp.sum(terms[0], -1, keepdims=True)
    for t in terms[1:]:
        total = total + jnp.sum(t, -1, keepdims=True)
    attention_output = None
    for t, value in zip(terms, value_blocks):
        part = jnp.einsum(
            "hqk,khd->qhd",
            (t / total).astype(jnp.bfloat16),
            split(value),
            preferred_element_type=jnp.float32,
        )
        attention_output = part if attention_output is None else attention_output + part
    attention_output = attention_output.astype(jnp.bfloat16).reshape(
        group_rows, heads_here * HEAD_SIZE
    )
    contract_product = (((1,), (1,)), ((), ()))
    own_blocks = [
        attention_output[:rows] if j == 0
        else swap(attention_output[j * rows : (j + 1) * rows], "uly", j)
        for j in range(uly_count)
    ]
    own_heads = jnp.concatenate(own_blocks, 1)

    weight_cols = jnp.concatenate(turn(out_parts, fsdp_id), 0)
    weight_full = jnp.concatenate(xor_gather(weight_cols, "uly"), 1)
    down_full = jnp.concatenate(xor_gather(adapter_down_map, "uly"), 1)

    narrow_projection = lax.dot_general(
        own_heads, down_full, contract_product, preferred_element_type=jnp.float32
    ).astype(jnp.bfloat16)
    adapter_result = jnp.dot(narrow_projection, adapter_up_map, preferred_element_type=jnp.float32)
    step_float = timestep_index[0].astype(jnp.float32)
    time_now = 1.0 - step_float / STEPS
    step_size = 1.0 / STEPS
    noise_std = noise_level * jnp.sqrt(time_now / (1.0 - time_now))
    drift_gain = 1.0 + noise_level**2 / 2.0
    ratio_gain = jnp.sqrt(step_size) * drift_gain / noise_std
    noise_f = sampler_noise[0].astype(jnp.float32)
    standard = noise_f + ratio_gain * adapter_result
    tok_pos = (uly_id * blk_count + blk_id) * rows + jnp.arange(rows, dtype=jnp.int32)
    tok_ok = (tok_pos < limit)[:, None]
    valid_len = limit.astype(jnp.float32)
    partial_log = jnp.sum(jnp.where(tok_ok, noise_f * noise_f - standard * standard, 0.0)) / (
        2.0 * valid_len * width
    )
    slots = jnp.where(jnp.arange(uly_count)[:, None] == uly_id, partial_log, 0.0)
    slots = jnp.broadcast_to(slots, (uly_count, HEAD_SIZE))
    slots = sum([swap(slots, "uly", j) for j in range(1, uly_count)], slots)
    by_uly = jnp.sum(slots, 0, keepdims=True)
    lines = jnp.where(jnp.arange(blk_count)[:, None] == blk_id, by_uly, 0.0)
    lines = sum([shift(lines, "blk", k) for k in range(1, blk_count)], lines)
    log_ratio = jnp.sum(lines, 0)[0]
    coef = (
        loss_scale
        * advantage[0]
        * jnp.exp(log_ratio)
        * ratio_gain
        / (fsdp_count * valid_len * width)
    )
    delta_gradient = (jnp.where(tok_ok, standard, 0.0) * coef).astype(jnp.bfloat16)
    first_axis = (((0,), (0,)), ((), ()))
    up_part = lax.dot_general(
        narrow_projection, delta_gradient, first_axis, preferred_element_type=jnp.float32
    )
    narrow_gradient = lax.dot_general(
        delta_gradient, adapter_up_map, contract_product, preferred_element_type=jnp.float32
    ).astype(jnp.bfloat16)
    down_part = lax.dot_general(
        narrow_gradient, own_heads, first_axis, preferred_element_type=jnp.float32
    )

    velocity = lax.dot_general(
        own_heads, weight_full, contract_product, preferred_element_type=jnp.float32
    )
    moved = current - step_size * (
        drift_gain * velocity + noise_level**2 * current / (2.0 * (1.0 - time_now))
    )
    next_latents = (moved + noise_std * jnp.sqrt(step_size) * noise_f).astype(jnp.bfloat16)[None]

    columns = width // uly_count
    local_columns = adapter_down_map.shape[1]
    shares = []
    for j in range(uly_count):
        at = jnp.bitwise_xor(uly_id, j) * columns
        shares.append(
            jnp.concatenate(
                [
                    lax.dynamic_slice_in_dim(up_part, at, columns, 1),
                    down_part[:, j * local_columns : (j + 1) * local_columns],
                ],
                1,
            )
        )
    share = xor_scatter(shares, "uly")
    piece = share.shape[0] // blk_count

    def rows_at(k):
        return lax.dynamic_slice_in_dim(share, lax.rem(blk_id + k, blk_count) * piece, piece, 0)

    mine = rows_at(0)
    for k in range(1, blk_count):
        mine = mine + shift(rows_at(k), "blk", blk_count - k)
    swapped = turn([mine] + [shift(mine, "fsdp", k) for k in range(1, fsdp_count)], fsdp_id)
    mine = sum(swapped[1:], swapped[0])
    whole = jnp.zeros_like(share)
    for k in range(blk_count):
        got = mine if k == 0 else shift(mine, "blk", k)
        whole = lax.dynamic_update_slice_in_dim(
            whole, got, lax.rem(blk_id + k, blk_count) * piece, 0
        )
    grad_down = whole[:, columns:]
    grad_up = jnp.zeros_like(up_part)
    for j, got in enumerate(xor_gather(whole[:, :columns], "uly")):
        grad_up = lax.dynamic_update_slice_in_dim(
            grad_up, got, jnp.bitwise_xor(uly_id, j) * columns, 1
        )
    return (next_latents, jnp.reshape(log_ratio, (1,)), grad_down, grad_up)


def solution(mesh):
    placed = (
        P("fsdp", ("uly", "blk"), None),
        P("fsdp", ("uly", "blk"), None),
        P(None, "fsdp", "uly"),
        P("fsdp", "uly"),
        P(None, "uly"),
        P(),
        P("fsdp"),
        P("fsdp"),
        P(),
    )
    return jax.shard_map(
        shards,
        mesh=mesh,
        in_specs=placed,
        out_specs=(P("fsdp", ("uly", "blk"), None), P("fsdp"), P(None, "uly"), P()),
        check_vma=False,
    )
```

```python
import math

import jax
import jax.numpy as jnp
from jax import lax
from jax.sharding import PartitionSpec as P

HEAD_SIZE = 128
STEPS = 16


noise_level = 0.7
loss_scale = 4194304.0
rms_eps = 1e-06


def shift(x, axis, by):
    n = lax.axis_size(axis)
    return lax.ppermute(x, axis, [((i + by) % n, i) for i in range(n)])


def swap(x, axis, bit):
    n = lax.axis_size(axis)
    return lax.ppermute(x, axis, [(i ^ bit, i) for i in range(n)])


def bits_of(axis):
    n = lax.axis_size(axis)
    assert n & (n - 1) == 0
    return [1 << i for i in reversed(range(n.bit_length() - 1))]


def xor_gather(x, axis, beside=None):
    blocks = {0: x}
    for bit in bits_of(axis):
        if beside is not None and bit == 1:
            blocks, _ = lax.optimization_barrier((blocks, beside))
        got = {j ^ bit: swap(v, axis, bit) for j, v in blocks.items()}
        blocks.update(got)
    return [blocks[j] for j in range(lax.axis_size(axis))]


def xor_scatter(blocks, axis):
    held = dict(enumerate(blocks))
    for bit in reversed(bits_of(axis)):
        got = {j ^ bit: swap(v, axis, bit) for j, v in held.items() if j & bit}
        held = {j: held[j] + got[j] for j in got}
    return held[0]


def turn(blocks, me):
    n = len(blocks)
    if n == 1:
        return blocks
    return [
        lax.select_n(
            lax.rem(c - me + n, n), *blocks
        ) if n > 2 else jnp.where(me == c, blocks[0], blocks[1])
        for c in range(n)
    ]


def shards(
    latents,
    sampler_noise,
    query_key_value_weight,
    output_weight,
    adapter_down_map,
    adapter_up_map,
    valid_token_count,
    advantage,
    timestep_index,
):
    fsdp_count = lax.axis_size("fsdp")
    uly_count = lax.axis_size("uly")
    blk_count = lax.axis_size("blk")
    fsdp_id = lax.axis_index("fsdp")
    uly_id = lax.axis_index("uly")
    blk_id = lax.axis_index("blk")
    out_piece = output_weight.shape[0] // blk_count
    piece_own = lax.dynamic_slice_in_dim(output_weight, blk_id * out_piece, out_piece, 0)
    query_weight, key_weight, value_weight = [query_key_value_weight[j] for j in range(3)]
    query_weight, key_weight, value_weight, piece_own, latents = lax.optimization_barrier(
        (query_weight, key_weight, value_weight, piece_own, latents)
    )

    def with_others(own):
        return [own] + [shift(own, "fsdp", k) for k in range(1, fsdp_count)]

    def ring(x):
        blocks = [x]
        for _ in range(blk_count - 1):
            blocks.append(shift(blocks[-1], "blk", 1))
        return blocks

    pieces = [shift(piece_own, "fsdp", k) for k in range(1, fsdp_count)]
    key_weights = with_others(key_weight)
    value_weights = with_others(value_weight)

    current = latents[0].astype(jnp.float32)
    rows = current.shape[0]
    width = current.shape[1]
    half = width // fsdp_count
    normed = (current * lax.rsqrt(jnp.mean(current * current, -1, keepdims=True) + rms_eps)).astype(
        jnp.bfloat16
    )
    gathered = jnp.concatenate(xor_gather(normed, "uly", key_weights), 0)
    halves = [
        lax.dynamic_slice_in_dim(gathered, lax.rem(fsdp_id + k, fsdp_count) * half, half, 1)
        for k in range(fsdp_count)
    ]

    def project(weights):
        total = None
        for part, weight in zip(halves, weights):
            term = jnp.dot(part, weight, preferred_element_type=jnp.float32)
            total = term if total is None else total + term
        return total.astype(jnp.bfloat16)

    out_parts = [output_weight]
    for got in pieces:
        part = jnp.zeros_like(output_weight)
        for k, block in enumerate(ring(got)):
            part = lax.dynamic_update_slice_in_dim(
                part, block, lax.rem(blk_id + k, blk_count) * out_piece, 0
            )
        out_parts.append(part)
    key_rows = project(key_weights)
    key_rows, *out_parts = lax.optimization_barrier((key_rows, *out_parts))
    key_blocks = ring(key_rows)
    value_rows = project(value_weights)
    value_rows, query_weight = lax.optimization_barrier((value_rows, query_weight))
    value_blocks = ring(value_rows)
    query_rows = project(with_others(query_weight))
    out_full = [jnp.concatenate(xor_gather(part, "uly"), 1) for part in out_parts]
    down_full = jnp.concatenate(xor_gather(adapter_down_map, "uly"), 1)

    limit = valid_token_count[0]
    group_rows = uly_count * rows
    row_index = jnp.arange(group_rows, dtype=jnp.int32)
    row_uly = jnp.bitwise_xor(row_index // rows, uly_id)
    heads_here = query_rows.shape[1] // HEAD_SIZE

    def split(x):
        return x.reshape(x.shape[0], heads_here, HEAD_SIZE)

    query_split = split(query_rows)
    masked = []
    oks = []
    for step in range(blk_count):
        from_blk = lax.rem(blk_id + step, blk_count)
        pos = (row_uly * blk_count + from_blk) * rows + row_index % rows
        ok = (pos < limit)[None, None, :]
        scores = jnp.einsum(
            "qhd,khd->hqk", query_split, split(key_blocks[step]), preferred_element_type=jnp.float32
        ) * (1.0 / math.sqrt(HEAD_SIZE))
        masked.append(jnp.where(ok, scores, -1e30))
        oks.append(ok)
    row_max = jnp.max(masked[0], -1, keepdims=True)
    for m in masked[1:]:
        row_max = jnp.maximum(row_max, jnp.max(m, -1, keepdims=True))
    terms = [jnp.where(ok, jnp.exp(m - row_max), 0.0) for m, ok in zip(masked, oks)]
    total = jnp.sum(terms[0], -1, keepdims=True)
    for t in terms[1:]:
        total = total + jnp.sum(t, -1, keepdims=True)
    total, down_full, *out_full = lax.optimization_barrier((total, down_full, *out_full))
    attention_output = None
    for t, value in zip(terms, value_blocks):
        part = jnp.einsum(
            "hqk,khd->qhd",
            (t / total).astype(jnp.bfloat16),
            split(value),
            preferred_element_type=jnp.float32,
        )
        attention_output = part if attention_output is None else attention_output + part
    attention_output = attention_output.astype(jnp.bfloat16).reshape(
        group_rows, heads_here * HEAD_SIZE
    )
    contract_product = (((1,), (1,)), ((), ()))
    own_blocks = [
        attention_output[:rows] if j == 0
        else swap(attention_output[j * rows : (j + 1) * rows], "uly", j)
        for j in range(uly_count)
    ]
    own_heads = jnp.concatenate(own_blocks, 1)

    narrow_projection = lax.dot_general(
        own_heads, down_full, contract_product, preferred_element_type=jnp.float32
    ).astype(jnp.bfloat16)
    adapter_result = jnp.dot(narrow_projection, adapter_up_map, preferred_element_type=jnp.float32)
    step_float = timestep_index[0].astype(jnp.float32)
    time_now = 1.0 - step_float / STEPS
    step_size = 1.0 / STEPS
    noise_std = noise_level * jnp.sqrt(time_now / (1.0 - time_now))
    drift_gain = 1.0 + noise_level**2 / 2.0
    ratio_gain = jnp.sqrt(step_size) * drift_gain / noise_std
    noise_f = sampler_noise[0].astype(jnp.float32)
    standard = noise_f + ratio_gain * adapter_result
    tok_pos = (uly_id * blk_count + blk_id) * rows + jnp.arange(rows, dtype=jnp.int32)
    tok_ok = (tok_pos < limit)[:, None]
    valid_len = limit.astype(jnp.float32)
    partial_log = jnp.sum(jnp.where(tok_ok, noise_f * noise_f - standard * standard, 0.0)) / (
        2.0 * valid_len * width
    )
    slots = jnp.where(jnp.arange(uly_count)[:, None] == uly_id, partial_log, 0.0)
    slots = jnp.broadcast_to(slots, (uly_count, HEAD_SIZE))
    slots = sum([swap(slots, "uly", j) for j in range(1, uly_count)], slots)
    by_uly = jnp.sum(slots, 0, keepdims=True)
    lines = jnp.where(jnp.arange(blk_count)[:, None] == blk_id, by_uly, 0.0)
    lines = sum([shift(lines, "blk", k) for k in range(1, blk_count)], lines)
    log_ratio = jnp.sum(lines, 0)[0]
    coef = (
        loss_scale
        * advantage[0]
        * jnp.exp(log_ratio)
        * ratio_gain
        / (fsdp_count * valid_len * width)
    )
    delta_gradient = (jnp.where(tok_ok, standard, 0.0) * coef).astype(jnp.bfloat16)
    first_axis = (((0,), (0,)), ((), ()))
    up_part = lax.dot_general(
        narrow_projection, delta_gradient, first_axis, preferred_element_type=jnp.float32
    )
    narrow_gradient = lax.dot_general(
        delta_gradient, adapter_up_map, contract_product, preferred_element_type=jnp.float32
    ).astype(jnp.bfloat16)
    down_part = lax.dot_general(
        narrow_gradient, own_heads, first_axis, preferred_element_type=jnp.float32
    )

    velocity = jnp.concatenate(
        turn(
            [
                lax.dot_general(own_heads, w, contract_product, preferred_element_type=jnp.float32)
                for w in out_full
            ],
            fsdp_id,
        ),
        1,
    )
    moved = current - step_size * (
        drift_gain * velocity + noise_level**2 * current / (2.0 * (1.0 - time_now))
    )
    next_latents = (moved + noise_std * jnp.sqrt(step_size) * noise_f).astype(jnp.bfloat16)[None]

    columns = width // uly_count
    local_columns = adapter_down_map.shape[1]
    shares = []
    for j in range(uly_count):
        at = jnp.bitwise_xor(uly_id, j) * columns
        shares.append(
            jnp.concatenate(
                [
                    lax.dynamic_slice_in_dim(up_part, at, columns, 1),
                    down_part[:, j * local_columns : (j + 1) * local_columns],
                ],
                1,
            )
        )
    share = xor_scatter(shares, "uly")
    piece = share.shape[0] // blk_count

    def rows_at(k):
        return lax.dynamic_slice_in_dim(share, lax.rem(blk_id + k, blk_count) * piece, piece, 0)

    mine = rows_at(0)
    for k in range(1, blk_count):
        mine = mine + shift(rows_at(k), "blk", blk_count - k)
    swapped = turn([mine] + [shift(mine, "fsdp", k) for k in range(1, fsdp_count)], fsdp_id)
    mine = sum(swapped[1:], swapped[0])
    whole = jnp.zeros_like(share)
    for k in range(blk_count):
        got = mine if k == 0 else shift(mine, "blk", k)
        whole = lax.dynamic_update_slice_in_dim(
            whole, got, lax.rem(blk_id + k, blk_count) * piece, 0
        )
    grad_down = whole[:, columns:]
    grad_up = jnp.zeros_like(up_part)
    for j, got in enumerate(xor_gather(whole[:, :columns], "uly")):
        grad_up = lax.dynamic_update_slice_in_dim(
            grad_up, got, jnp.bitwise_xor(uly_id, j) * columns, 1
        )
    return (next_latents, jnp.reshape(log_ratio, (1,)), grad_down, grad_up)


def solution(mesh):
    placed = (
        P("fsdp", ("uly", "blk"), None),
        P("fsdp", ("uly", "blk"), None),
        P(None, "fsdp", "uly"),
        P("fsdp", "uly"),
        P(None, "uly"),
        P(),
        P("fsdp"),
        P("fsdp"),
        P(),
    )
    return jax.shard_map(
        shards,
        mesh=mesh,
        in_specs=placed,
        out_specs=(P("fsdp", ("uly", "blk"), None), P("fsdp"), P(None, "uly"), P()),
        check_vma=False,
    )
```

```python
import math

import jax
import jax.numpy as jnp
from jax import lax
from jax.sharding import PartitionSpec as P

HEAD_SIZE = 128
STEPS = 16


noise_level = 0.7
loss_scale = 4194304.0
rms_eps = 1e-06


def shift(x, axis, by):
    n = lax.axis_size(axis)
    return lax.ppermute(x, axis, [((i + by) % n, i) for i in range(n)])


def swap(x, axis, bit):
    n = lax.axis_size(axis)
    return lax.ppermute(x, axis, [(i ^ bit, i) for i in range(n)])


def bits_of(axis):
    n = lax.axis_size(axis)
    assert n & (n - 1) == 0
    return [1 << i for i in reversed(range(n.bit_length() - 1))]


def xor_gather(x, axis, beside=None):
    blocks = {0: x}
    for bit in bits_of(axis):
        if beside is not None and bit == 1:
            blocks, _ = lax.optimization_barrier((blocks, beside))
        got = {j ^ bit: swap(v, axis, bit) for j, v in blocks.items()}
        blocks.update(got)
    return [blocks[j] for j in range(lax.axis_size(axis))]


def xor_scatter(blocks, axis):
    held = dict(enumerate(blocks))
    for bit in reversed(bits_of(axis)):
        got = {j ^ bit: swap(v, axis, bit) for j, v in held.items() if j & bit}
        held = {j: held[j] + got[j] for j in got}
    return held[0]


def turn(blocks, me):
    n = len(blocks)
    if n == 1:
        return blocks
    return [
        lax.select_n(
            lax.rem(c - me + n, n), *blocks
        ) if n > 2 else jnp.where(me == c, blocks[0], blocks[1])
        for c in range(n)
    ]


def shards(
    latents,
    sampler_noise,
    query_key_value_weight,
    output_weight,
    adapter_down_map,
    adapter_up_map,
    valid_token_count,
    advantage,
    timestep_index,
):
    fsdp_count = lax.axis_size("fsdp")
    uly_count = lax.axis_size("uly")
    blk_count = lax.axis_size("blk")
    fsdp_id = lax.axis_index("fsdp")
    uly_id = lax.axis_index("uly")
    blk_id = lax.axis_index("blk")
    query_weight, key_weight, value_weight = [query_key_value_weight[j] for j in range(3)]
    query_weight, key_weight, value_weight, latents = lax.optimization_barrier(
        (query_weight, key_weight, value_weight, latents)
    )

    def with_others(own):
        return [own] + [shift(own, "fsdp", k) for k in range(1, fsdp_count)]

    def ring(x):
        blocks = [x]
        for _ in range(blk_count - 1):
            blocks.append(shift(blocks[-1], "blk", 1))
        return blocks

    key_weights = with_others(key_weight)

    current = latents[0].astype(jnp.float32)
    rows = current.shape[0]
    width = current.shape[1]
    half = width // fsdp_count
    normed = (current * lax.rsqrt(jnp.mean(current * current, -1, keepdims=True) + rms_eps)).astype(
        jnp.bfloat16
    )
    gathered = jnp.concatenate(xor_gather(normed, "uly", key_weights), 0)
    halves = [
        lax.dynamic_slice_in_dim(gathered, lax.rem(fsdp_id + k, fsdp_count) * half, half, 1)
        for k in range(fsdp_count)
    ]

    def project(weights):
        total = None
        for part, weight in zip(halves, weights):
            term = jnp.dot(part, weight, preferred_element_type=jnp.float32)
            total = term if total is None else total + term
        return total.astype(jnp.bfloat16)

    key_rows = project(key_weights)
    key_rows, value_weight = lax.optimization_barrier((key_rows, value_weight))
    key_blocks = ring(key_rows)
    value_rows = project(with_others(value_weight))
    value_rows, query_weight, later_weight = lax.optimization_barrier(
        (value_rows, query_weight, output_weight)
    )
    value_blocks = ring(value_rows)
    query_rows = project(with_others(query_weight))
    out_parts = [output_weight] + with_others(later_weight)[1:]
    out_full = [xor_gather(part, "uly") for part in out_parts]
    down_full = jnp.concatenate(xor_gather(adapter_down_map, "uly"), 1)

    limit = valid_token_count[0]
    group_rows = uly_count * rows
    row_index = jnp.arange(group_rows, dtype=jnp.int32)
    row_uly = jnp.bitwise_xor(row_index // rows, uly_id)
    heads_here = query_rows.shape[1] // HEAD_SIZE

    def split(x):
        return x.reshape(x.shape[0], heads_here, HEAD_SIZE)

    query_split = split(query_rows)
    masked = []
    oks = []
    for step in range(blk_count):
        from_blk = lax.rem(blk_id + step, blk_count)
        pos = (row_uly * blk_count + from_blk) * rows + row_index % rows
        ok = (pos < limit)[None, None, :]
        scores = jnp.einsum(
            "qhd,khd->hqk", query_split, split(key_blocks[step]), preferred_element_type=jnp.float32
        ) * (1.0 / math.sqrt(HEAD_SIZE))
        masked.append(jnp.where(ok, scores, -1e30))
        oks.append(ok)
    row_max = jnp.max(masked[0], -1, keepdims=True)
    for m in masked[1:]:
        row_max = jnp.maximum(row_max, jnp.max(m, -1, keepdims=True))
    terms = [jnp.where(ok, jnp.exp(m - row_max), 0.0) for m, ok in zip(masked, oks)]
    total = jnp.sum(terms[0], -1, keepdims=True)
    for t in terms[1:]:
        total = total + jnp.sum(t, -1, keepdims=True)
    attention_output = None
    for t, value in zip(terms, value_blocks):
        part = jnp.einsum(
            "hqk,khd->qhd",
            (t / total).astype(jnp.bfloat16),
            split(value),
            preferred_element_type=jnp.float32,
        )
        attention_output = part if attention_output is None else attention_output + part
    attention_output = attention_output.astype(jnp.bfloat16).reshape(
        group_rows, heads_here * HEAD_SIZE
    )
    attention_output, down_full, out_full = lax.optimization_barrier(
        (attention_output, down_full, out_full)
    )
    contract_product = (((1,), (1,)), ((), ()))
    own_blocks = [
        attention_output[:rows] if j == 0
        else swap(attention_output[j * rows : (j + 1) * rows], "uly", j)
        for j in range(uly_count)
    ]
    own_heads = jnp.concatenate(own_blocks, 1)

    narrow_projection = lax.dot_general(
        own_heads, down_full, contract_product, preferred_element_type=jnp.float32
    ).astype(jnp.bfloat16)
    adapter_result = jnp.dot(narrow_projection, adapter_up_map, preferred_element_type=jnp.float32)
    step_float = timestep_index[0].astype(jnp.float32)
    time_now = 1.0 - step_float / STEPS
    step_size = 1.0 / STEPS
    noise_std = noise_level * jnp.sqrt(time_now / (1.0 - time_now))
    drift_gain = 1.0 + noise_level**2 / 2.0
    ratio_gain = jnp.sqrt(step_size) * drift_gain / noise_std
    noise_f = sampler_noise[0].astype(jnp.float32)
    standard = noise_f + ratio_gain * adapter_result
    tok_pos = (uly_id * blk_count + blk_id) * rows + jnp.arange(rows, dtype=jnp.int32)
    tok_ok = (tok_pos < limit)[:, None]
    valid_len = limit.astype(jnp.float32)
    partial_log = jnp.sum(jnp.where(tok_ok, noise_f * noise_f - standard * standard, 0.0)) / (
        2.0 * valid_len * width
    )
    slots = jnp.where(jnp.arange(uly_count)[:, None] == uly_id, partial_log, 0.0)
    slots = jnp.broadcast_to(slots, (uly_count, HEAD_SIZE))
    slots = sum([swap(slots, "uly", j) for j in range(1, uly_count)], slots)
    by_uly = jnp.sum(slots, 0, keepdims=True)
    lines = jnp.where(jnp.arange(blk_count)[:, None] == blk_id, by_uly, 0.0)
    lines = sum([shift(lines, "blk", k) for k in range(1, blk_count)], lines)
    log_ratio = jnp.sum(lines, 0)[0]
    coef = (
        loss_scale
        * advantage[0]
        * jnp.exp(log_ratio)
        * ratio_gain
        / (fsdp_count * valid_len * width)
    )
    delta_gradient = (jnp.where(tok_ok, standard, 0.0) * coef).astype(jnp.bfloat16)
    first_axis = (((0,), (0,)), ((), ()))
    up_part = lax.dot_general(
        narrow_projection, delta_gradient, first_axis, preferred_element_type=jnp.float32
    )
    narrow_gradient = lax.dot_general(
        delta_gradient, adapter_up_map, contract_product, preferred_element_type=jnp.float32
    ).astype(jnp.bfloat16)
    down_part = lax.dot_general(
        narrow_gradient, own_heads, first_axis, preferred_element_type=jnp.float32
    )

    velocity = jnp.concatenate(
        turn(
            [
                sum(
                    lax.dot_general(a, w, contract_product, preferred_element_type=jnp.float32)
                    for a, w in zip(own_blocks, part)
                )
                for part in out_full
            ],
            fsdp_id,
        ),
        1,
    )
    moved = current - step_size * (
        drift_gain * velocity + noise_level**2 * current / (2.0 * (1.0 - time_now))
    )
    next_latents = (moved + noise_std * jnp.sqrt(step_size) * noise_f).astype(jnp.bfloat16)[None]

    columns = width // uly_count
    local_columns = adapter_down_map.shape[1]
    shares = []
    for j in range(uly_count):
        at = jnp.bitwise_xor(uly_id, j) * columns
        shares.append(
            jnp.concatenate(
                [
                    lax.dynamic_slice_in_dim(up_part, at, columns, 1),
                    down_part[:, j * local_columns : (j + 1) * local_columns],
                ],
                1,
            )
        )
    share = xor_scatter(shares, "uly")
    piece = share.shape[0] // blk_count

    def rows_at(k):
        return lax.dynamic_slice_in_dim(share, lax.rem(blk_id + k, blk_count) * piece, piece, 0)

    mine = rows_at(0)
    for k in range(1, blk_count):
        mine = mine + shift(rows_at(k), "blk", blk_count - k)
    swapped = turn([mine] + [shift(mine, "fsdp", k) for k in range(1, fsdp_count)], fsdp_id)
    mine = sum(swapped[1:], swapped[0])
    whole = jnp.zeros_like(share)
    for k in range(blk_count):
        got = mine if k == 0 else shift(mine, "blk", k)
        whole = lax.dynamic_update_slice_in_dim(
            whole, got, lax.rem(blk_id + k, blk_count) * piece, 0
        )
    grad_down = whole[:, columns:]
    grad_up = jnp.zeros_like(up_part)
    for j, got in enumerate(xor_gather(whole[:, :columns], "uly")):
        grad_up = lax.dynamic_update_slice_in_dim(
            grad_up, got, jnp.bitwise_xor(uly_id, j) * columns, 1
        )
    return (next_latents, jnp.reshape(log_ratio, (1,)), grad_down, grad_up)


def solution(mesh):
    placed = (
        P("fsdp", ("uly", "blk"), None),
        P("fsdp", ("uly", "blk"), None),
        P(None, "fsdp", "uly"),
        P("fsdp", "uly"),
        P(None, "uly"),
        P(),
        P("fsdp"),
        P("fsdp"),
        P(),
    )
    return jax.shard_map(
        shards,
        mesh=mesh,
        in_specs=placed,
        out_specs=(P("fsdp", ("uly", "blk"), None), P("fsdp"), P(None, "uly"), P()),
        check_vma=False,
    )
```
